128 devices in a mesh: obj: 8 (over z, core), pos: 16 (over y, x).
Axes of the slice: x: 4, y: 4, z: 4, core: 2. Of those that a mesh axis runs over, the one named last changes fastest.
Arguments:
- object_field: float32 [2, 4096, 8192], P(None, 'obj', 'pos'), may hold values from -5 to 5
- probe: float32 [2, 512, 512], replicated, may hold values from -5 to 5
- amplitudes: float32 [128, 512, 512], P(('obj', 'pos')), may hold values from 0.1 to 3
- offsets: int32 [128, 2], P(('obj', 'pos')), may hold values from 0 to 7680, as said below
Outputs:
- new_object: float32 [2, 4096, 8192], P(None, 'obj', 'pos')
- new_probe: float32 [2, 512, 512], replicated
The draws below stay inside these ranges and needn't reach their ends.
Inputs may be any that keep to these rules, and one draw needn't show every extreme that they name: `offsets`: position k's patch starts in the tile of device k // 1 of obj+pos: its row lies in [o * 512, (o + 1) * 512) and its column in [p * 512, (p + 1) * 512) with o = k // 16 and p = (k) % 16, except that row is at most 3584 and column at most 7680, so every patch lies inside the object.
All inputs are finite; a program needn't handle non-finite values.
Results may differ from the reference program's by a relative error of at most 0.012.
The reference program's roundings to bfloat16 on the way count: a program that leaves them out, or rounds other values in their place, can miss the bound.
Values sent between devices are 32-bit elements; how exact they have to be, the bound alone decides.
No kernel may reach another device: no remote copies, remote signals or barrier semaphores. Data moves between devices by JAX's collectives and lax.ppermute only.
A program may use at most 128 MiB of HBM per device.

```python
import math
import jax
import jax.numpy as jnp
from jax import lax

F = 512
TILE = 512
POS_DEV = 1
POSITIONS = 128
NOB = 4096
NOBX = 8192
N_POS = 16


def draw_offsets(key, part):
    key = jax.random.fold_in(key, 11)
    key_rows, key_cols = jax.random.split(key)
    index = jnp.arange(POSITIONS, dtype=jnp.int32)
    device = index // POS_DEV
    tile_row = device // N_POS
    tile_col = device % N_POS
    rows = tile_row * TILE + jax.random.randint(key_rows, (POSITIONS,), 0, TILE, dtype=jnp.int32)
    cols = tile_col * TILE + jax.random.randint(key_cols, (POSITIONS,), 0, TILE, dtype=jnp.int32)
    rows = jnp.minimum(rows, NOB - F)
    cols = jnp.minimum(cols, NOBX - F)
    return jnp.stack([rows, cols], axis=1).astype(jnp.int32)


def shard_levels(stream_key, shape, pieces, low, largest):
    gain = 1.0
    for position, shards_of in pieces:
        heights = jax.random.uniform(jax.random.fold_in(jax.random.fold_in(stream_key, 6), position), (shards_of,), jnp.float32, low / len(pieces), largest / len(pieces))
        gain = gain * jnp.repeat(jnp.exp(heights), shape[position] // shards_of).reshape((-1,) + (1,) * (len(shape) - 1 - position))
    return gain


def normal_values(own_key, shape, deviation, most, cuts=(), kind=jnp.bfloat16):
    gain = shard_levels(own_key, shape, cuts, -0.22, 0.18) if cuts else 1.0
    values = jax.random.normal(own_key, shape, jnp.float32) * deviation * gain
    return jnp.minimum(jnp.maximum(values, -most), most).astype(kind)


def setup_inputs(seed: int = 0) -> dict:
    key_of = jax.random.split(jax.random.key(seed), 5)
    object_field = normal_values(key_of[0], (2, NOB, NOBX), 0.7, 5.0, ((1, 8), (2, 16)), jnp.float32)
    probe = normal_values(key_of[1], (2, F, F), 0.7, 5.0, (), jnp.float32)
    amplitudes = jnp.clip(jnp.exp(math.log(3.0) - 3.4011974 * jax.random.uniform(key_of[2], (POSITIONS, F, F), jnp.float32) ** shard_levels(key_of[2], (POSITIONS, F, F), ((0, 128),), -0.2, 0.2)), 0.1, 3.0)
    offsets = draw_offsets(jax.random.fold_in(key_of[4], 71), 0)
    return dict(object_field=object_field, probe=probe, amplitudes=amplitudes, offsets=offsets)


def dft_tables(size):
    idx = jnp.arange(size, dtype=jnp.int32)
    turns = idx[:, None] * idx[None, :] % size
    angle = turns.astype(jnp.float32) * (2.0 * math.pi / size)
    scale = 1.0 / math.sqrt(size)
    return ((jnp.cos(angle) * scale).astype(jnp.bfloat16), (-jnp.sin(angle) * scale).astype(jnp.bfloat16))

def right_mul(frames, table):
    return jnp.einsum('prc,ck->prk', frames.astype(jnp.float32), table.astype(jnp.float32))

def left_mul(table, frames):
    return jnp.einsum('jr,prc->pjc', table.astype(jnp.float32), frames.astype(jnp.float32))

def fourier_step(patch_real, patch_imag, probe_real, probe_imag, amps, table_re, table_im):
    psi_re = (probe_real * patch_real - probe_imag * patch_imag).astype(jnp.bfloat16)
    psi_im = (probe_real * patch_imag + probe_imag * patch_real).astype(jnp.bfloat16)
    half_re = (right_mul(psi_re, table_re) - right_mul(psi_im, table_im)).astype(jnp.bfloat16)
    half_im = (right_mul(psi_re, table_im) + right_mul(psi_im, table_re)).astype(jnp.bfloat16)
    spec_re = left_mul(table_re, half_re) - left_mul(table_im, half_im)
    spec_im = left_mul(table_re, half_im) + left_mul(table_im, half_re)
    magnitude = jnp.sqrt(spec_re * spec_re + spec_im * spec_im)
    factor = amps / jnp.maximum(magnitude, 0.25) - 1.0
    change_re = (factor * spec_re).astype(jnp.bfloat16)
    change_im = (factor * spec_im).astype(jnp.bfloat16)
    back_re = (left_mul(table_re, change_re) + left_mul(table_im, change_im)).astype(jnp.bfloat16)
    back_im = (left_mul(table_re, change_im) - left_mul(table_im, change_re)).astype(jnp.bfloat16)
    err_re = right_mul(back_re, table_re) + right_mul(back_im, table_im)
    err_im = right_mul(back_im, table_re) - right_mul(back_re, table_im)
    return (err_re, err_im)

def reference(object_field, probe, amplitudes, offsets):
    table_re, table_im = dft_tables(F)
    probe_real = probe[0]
    probe_imag = probe[1]
    power = probe_real * probe_real + probe_imag * probe_imag

    def visit(carry, item):
        numer, light, pnum, pden = carry
        corner, amps = item
        row = corner[0].astype(jnp.int32)
        col = corner[1].astype(jnp.int32)
        zero = jnp.int32(0)
        patch = lax.dynamic_slice(object_field, (zero, row, col), (2, F, F))
        err_re, err_im = fourier_step(patch[0][None], patch[1][None], probe_real, probe_imag, amps[None], table_re, table_im)
        err_re = err_re[0]
        err_im = err_im[0]
        grad = jnp.stack([probe_real * err_re + probe_imag * err_im, probe_real * err_im - probe_imag * err_re])
        block = lax.dynamic_slice(numer, (zero, row, col), (2, F, F)) + grad
        numer = lax.dynamic_update_slice(numer, block, (zero, row, col))
        lblock = lax.dynamic_slice(light, (row, col), (F, F)) + power
        light = lax.dynamic_update_slice(light, lblock, (row, col))
        pgrad = jnp.stack([patch[0] * err_re + patch[1] * err_im, patch[0] * err_im - patch[1] * err_re])
        pnum = pnum + pgrad
        pden = pden + patch[0] * patch[0] + patch[1] * patch[1]
        return ((numer, light, pnum, pden), None)
    start = (jnp.zeros((2, NOB, NOBX), jnp.float32), jnp.zeros((NOB, NOBX), jnp.float32), jnp.zeros((2, F, F), jnp.float32), jnp.zeros((F, F), jnp.float32))
    (numer, light, pnum, pden), unused = lax.scan(visit, start, (offsets, amplitudes))
    new_object = object_field + numer / (light + 1.0)
    beta = 0.5 * math.sqrt(POSITIONS)
    new_probe = probe + beta * pnum / (pden + 1.0)
    return (new_object, new_probe)
```

```python
import functools
import math

import jax
import jax.numpy as jnp
import numpy as np
from jax import lax
from jax.experimental import pallas as pl
from jax.experimental.pallas import tpu as pltpu
from jax.sharding import PartitionSpec as P

F = 512
CHUNKS = 4
R = F // CHUNKS
Y = X = Z = 4
HALF, QUARTER, SIXTEENTH = F // 2, F // 8, F // 32
F32, BF16 = jnp.float32, jnp.bfloat16
VMEM = pl.BlockSpec(memory_space=pltpu.VMEM)
SMEM = pl.BlockSpec(memory_space=pltpu.SMEM)

ROW, COL, ROW_T, COL_T, CORE, AT_Y, AT_Z, TOUCH = 0, 1, 2, 3, 4, 5, 6, 7


def dft_tables():
    idx = np.arange(F)
    angle = (idx[:, None] * idx[None, :] % F) * (2.0 * math.pi / F)
    scale = 1.0 / math.sqrt(F)
    return (
        jnp.asarray((np.cos(angle) * scale).astype(np.float32)).astype(BF16),
        jnp.asarray((-np.sin(angle) * scale).astype(np.float32)).astype(BF16),
    )


def call(kernel, out_shapes, args, specs=None, scratch=(), limit=48, **params):
    return pl.pallas_call(
        kernel,
        out_shape=[jax.ShapeDtypeStruct(s, d) for s, d in out_shapes],
        in_specs=specs or [SMEM] + [VMEM] * (len(args) - 1),
        out_specs=[VMEM] * len(out_shapes),
        scratch_shapes=list(scratch),
        compiler_params=pltpu.CompilerParams(vmem_limit_bytes=limit * 2**20, **params),
    )(*args)


def iota(shape, dim):
    return lax.broadcasted_iota(jnp.int32, shape, dim)


def back_by(shift):
    return jnp.bitwise_and(F - shift, F - 1)


def prep_kernel(s, wr, wi, probe, cf, rf, rb, cb, turned):
    r, c = s[ROW], s[COL]
    w_re, w_im = wr[...].astype(F32), wi[...].astype(F32)
    for out, axis, shift, sign in ((cf, 0, c, 1), (rf, 1, r, -1), (rb, 0, r, 1), (cb, 1, c, -1)):
        re = pltpu.roll(w_re, shift, axis).astype(BF16)
        im = (pltpu.roll(w_im, shift, axis) * sign).astype(BF16)
        out[:F, :F] = re
        out[F:, F:] = re
        out[:F, F:] = im
        out[F:, :F] = -im
    for k in range(2):
        turned[k] = pltpu.roll(pltpu.roll(probe[k], r, 0), c, 1)


def corner(s, which):
    return s[TOUCH + 2 * which], s[TOUCH + 2 * which + 1]


def touch_mask(which, r, c):
    row, col = iota((F, F), 0), iota((F, F), 1)
    inside_rows = row >= r if which < 2 else row < r
    inside_cols = col >= c if which % 2 == 0 else col < c
    return jnp.logical_and(inside_rows, inside_cols)


def probe_light_kernel(s, obj, keep, send):
    value = obj[0] * obj[0] + obj[1] * obj[1]
    total = jnp.zeros((F, F), F32)
    for which in range(4):
        r, c = corner(s, which)
        part = jnp.where(touch_mask(which, r, c), value, 0.0)
        total += pltpu.roll(pltpu.roll(part, back_by(c), 1), back_by(r + s[CORE] * HALF), 0)
    keep[...] = total[:HALF]
    send[...] = total[HALF:]


def light_kernel(s, probe, out):
    power = probe[0] * probe[0] + probe[1] * probe[1]
    total = jnp.zeros((F, F), F32)
    for which in range(4):
        r, c = corner(s, which)
        part = pltpu.roll(pltpu.roll(power, r, 0), c, 1)
        total += jnp.where(touch_mask(which, r, c), part, 0.0)
    out[...] = total


def half_kernel(first, s, obj, below, beside, turned, cf, patch, half):
    r, c, odd = s[ROW], s[COL], s[CORE] == 1
    row = iota((R, F), 0) + first
    col = iota((R, F), 1)
    low, high = jnp.where(odd, 0, c), jnp.where(odd, c, F)
    here = jnp.logical_and(col >= low, col < high)
    m = [jnp.where(here, jnp.where(row >= r, obj[k], below[k]), beside[k]) for k in range(2)]
    for k in range(2):
        patch[k] = m[k]
    psi_re = (turned[0] * m[0] - turned[1] * m[1]).astype(BF16)
    psi_im = (turned[0] * m[1] + turned[1] * m[0]).astype(BF16)
    out = jnp.dot(jnp.concatenate([psi_re, psi_im], axis=1), cf[...], preferred_element_type=F32)
    half[0] = out[:, :F].astype(BF16)
    half[1] = out[:, F:].astype(BF16)


def fourier_kernel(s, *refs):
    halves, patches = refs[:CHUNKS], refs[CHUNKS : 2 * CHUNKS]
    rf, rb, cb, amps, amps_moved, turned = refs[2 * CHUNKS : 2 * CHUNKS + 6]
    grads = refs[2 * CHUNKS + 6 : 3 * CHUNKS + 6]
    keep, send, stack, change, back, numer = refs[3 * CHUNKS + 6 :]
    r, c, odd = s[ROW], s[COL], s[CORE] == 1
    for i in range(CHUNKS):
        for k in range(2):
            stack[k * F + i * R : k * F + (i + 1) * R] = halves[i][k]
    wide = 256
    for j in range(0, F, wide):
        at = slice(j, j + wide)
        spec = jnp.dot(rf[...], stack[:, at], preferred_element_type=F32)
        re, im = spec[:F], spec[F:]
        a = jnp.where(odd, amps_moved[0, :, at], amps[0, :, at])
        factor = a / jnp.maximum(jnp.sqrt(re * re + im * im), 0.25) - 1.0
        change[:F, at] = (factor * re).astype(BF16)
        change[F:, at] = (factor * im).astype(BF16)
    for j in range(0, F, wide):
        at = slice(j, j + wide)
        out = jnp.dot(rb[...], change[:, at], preferred_element_type=F32)
        back[:, j : j + wide] = out[:F].astype(BF16)
        back[:, F + j : F + j + wide] = out[F:].astype(BF16)
    for i in range(CHUNKS):
        at = slice(i * R, (i + 1) * R)
        err = jnp.dot(back[at], cb[...], preferred_element_type=F32)
        re, im = err[:, :F], err[:, F:]
        p_re, p_im = turned[0, at], turned[1, at]
        grads[i][0] = p_re * re + p_im * im
        grads[i][1] = p_re * im - p_im * re
        m_re, m_im = patches[i][0], patches[i][1]
        numer[0, at] = pltpu.roll(m_re * re + m_im * im, back_by(c), 1)
        numer[1, at] = pltpu.roll(m_re * im - m_im * re, back_by(c), 1)
    for k in range(2):
        turned_back = pltpu.roll(numer[k], back_by(r + s[CORE] * HALF), 0)
        keep[k] = turned_back[:HALF]
        send[k] = turned_back[HALF:]


def split_kernel(axis, parts, rows, s, *refs):
    ins, outs, held = refs[: sum(parts)], refs[sum(parts) : -1], refs[-1]
    at, first = 0, 0
    for count in parts:
        total = ins[at][...]
        for ref in ins[at + 1 : at + count]:
            total = total + ref[...]
        planes = total.shape[0] if total.ndim == 3 else 1
        held[first : first + planes] = total.reshape((planes,) + total.shape[-2:])
        at, first = at + count, first + planes
    for j in range(4):
        block = jnp.bitwise_and(s[axis] + j, 3)
        outs[j][...] = held[:, pl.ds(pl.multiple_of(block * rows, rows), rows), :]


def join_kernel(axis, rows, s, *refs):
    for j in range(4):
        block = jnp.bitwise_and(s[axis] - j, 3)
        refs[4][:, pl.ds(pl.multiple_of(block * rows, rows), rows), :] = refs[j][...]


def update_kernel(beta, s, a, b, c, d, probe, out):
    total = a[...] + b[...] + c[...] + d[...]
    out[...] = probe[...] + beta * total[:2] / (total[2:3] + 1.0)


def turn(value, along, steps):
    if along == "z":
        return lax.ppermute(value, "obj", [(o, (o + 2 * steps) % (2 * Z)) for o in range(2 * Z)])
    pairs = []
    for y in range(Y):
        for x in range(X):
            to = (y, (x + steps) % X) if along == "x" else ((y + steps) % Y, x)
            pairs.append((y * X + x, to[0] * X + to[1]))
    return lax.ppermute(value, "pos", pairs)


def swap(value):
    return lax.ppermute(value, "obj", [(o, o ^ 1) for o in range(2 * Z)])


def shifted(value, steps):
    n = 2 * Z
    return lax.ppermute(value, "obj", [(o, o + steps) for o in range(n) if 0 <= o + steps < n])


def x_pairs(odd_only=False):
    n = Y * X
    pairs = [(o * n + p, o * n + (p + 1) % n) for o in range(1, 2 * Z, 2) for p in range(n)]
    if not odd_only:
        pairs += [(o * n + p, o * n + p - 1) for o in range(0, 2 * Z, 2) for p in range(1, n)]
    return pairs


def toward(value, odd_only=False):
    return lax.ppermute(value, ("obj", "pos"), x_pairs(odd_only))


def homeward(value):
    return lax.ppermute(value, ("obj", "pos"), [(b, a) for a, b in x_pairs()])


def body(object_field, probe, amplitudes, offsets):
    row_index = lax.axis_index("obj")
    col_index = lax.axis_index("pos")
    core, z = row_index % 2, row_index // 2
    y = col_index // X
    own = offsets[0] - jnp.stack([row_index * F, col_index * F])
    n = Y * X
    left = lax.ppermute(own, "pos", [(p, (p + 1) % n) for p in range(n)])
    above = shifted(jnp.concatenate([own, left]), 1)
    odd = core == 1
    mine, target = jnp.where(odd, left, own), jnp.where(odd, own, left)
    s = jnp.concatenate([mine, target, jnp.stack([core, y, z]), own, left, above]).astype(jnp.int32)

    col = jnp.arange(F, dtype=jnp.int32)[None, :]
    here = (col >= jnp.where(odd, 0, mine[1])) & (col < jnp.where(odd, mine[1], F))
    there = (col >= jnp.where(odd, target[1], 0)) & (col < jnp.where(odd, F, target[1]))
    rows = [jnp.arange(i * R, (i + 1) * R, dtype=jnp.int32)[:, None] for i in range(CHUNKS)]

    tiles = [object_field[:, i * R : (i + 1) * R] for i in range(CHUNKS)]
    below = [shifted(t, -1) for t in tiles]
    amps_moved = toward(amplitudes, odd_only=True)
    beside = [
        toward(jnp.where(rows[i] >= target[0], tiles[i], below[i])) for i in range(CHUNKS)
    ]

    wr, wi = dft_tables()
    square = ((2 * F, 2 * F), BF16)
    cf, rf, rb, cb, turned = call(
        prep_kernel, [square] * 4 + [((2, F, F), F32)], (s, wr, wi, probe)
    )
    pl_keep, pl_send = call(probe_light_kernel, [((HALF, F), F32)] * 2, (s, object_field))
    pl_got = swap(pl_send)
    pl_blocks = call(
        functools.partial(split_kernel, AT_Y, (2,), QUARTER),
        [((1, QUARTER, F), F32)] * 4,
        (s, pl_keep, pl_got),
        scratch=[pltpu.VMEM((1, HALF, F), F32)],
    )
    pl_parts = [pl_blocks[0]] + [turn(pl_blocks[j], "y", j) for j in (1, 2, 3)]

    patches, halves = [], []
    for i in range(CHUNKS):
        chunk = pl.BlockSpec((2, R, F), lambda g, i=i: (0, i, 0))
        whole = pl.BlockSpec((2, R, F), lambda g: (0, 0, 0))
        table = pl.BlockSpec((2 * F, 2 * F), lambda g: (0, 0))
        patch, half = pl.pallas_call(
            functools.partial(half_kernel, i * R),
            grid=(1,),
            out_shape=[
                jax.ShapeDtypeStruct((2, R, F), F32),
                jax.ShapeDtypeStruct((2, R, F), BF16),
            ],
            in_specs=[SMEM, chunk, whole, whole, chunk, table],
            out_specs=[whole, whole],
            compiler_params=pltpu.CompilerParams(vmem_limit_bytes=40 * 2**20),
        )(s, object_field, below[i], beside[i], turned, cf)
        patches.append(patch)
        halves.append(half)

    *grads, pn_keep, pn_send = call(
        fourier_kernel,
        [((2, R, F), F32)] * CHUNKS + [((2, HALF, F), F32)] * 2,
        (s, *halves, *patches, rf, rb, cb, amplitudes, amps_moved, turned),
        scratch=[
            pltpu.VMEM((2 * F, F), BF16),
            pltpu.VMEM((2 * F, F), BF16),
            pltpu.VMEM((F, 2 * F), BF16),
            pltpu.VMEM((2, F, F), F32),
        ],
    )

    (light,) = call(light_kernel, [((F, F), F32)], (s, probe))
    moved = [homeward(g) for g in grads]
    down = []
    for i in range(CHUNKS):
        mine_down = jnp.where(here & (rows[i] < mine[0]), grads[i], 0.0)
        moved_down = jnp.where(there & (rows[i] < target[0]), moved[i], 0.0)
        down.append(shifted(mine_down + moved_down, 1))

    pn_got = swap(pn_send)
    pn_blocks = call(
        functools.partial(split_kernel, AT_Y, (2,), QUARTER),
        [((2, QUARTER, F), F32)] * 4,
        (s, pn_keep, pn_got),
        scratch=[pltpu.VMEM((2, HALF, F), F32)],
    )
    pn_parts = [pn_blocks[0]] + [turn(pn_blocks[j], "y", j) for j in (1, 2, 3)]
    blocks = call(
        functools.partial(split_kernel, AT_Z, (4, 4), SIXTEENTH),
        [((3, SIXTEENTH, F), F32)] * 4,
        (s, *pn_parts, *pl_parts),
        scratch=[pltpu.VMEM((3, QUARTER, F), F32)],
    )
    parts = [blocks[0]] + [turn(blocks[j], "z", j) for j in (1, 2, 3)]
    share = parts[0] + parts[1] + parts[2] + parts[3]
    shares = [share] + [turn(share, "x", j) for j in (1, 2, 3)]
    beta = 0.5 * math.sqrt(Y * X * 2 * Z)
    start = core * HALF + y * QUARTER + z * SIXTEENTH
    probe_rows = lax.dynamic_slice(probe, (0, start, 0), (2, SIXTEENTH, F))
    (fresh,) = call(
        functools.partial(update_kernel, beta),
        [((2, SIXTEENTH, F), F32)],
        (s, *shares, probe_rows),
    )
    for along, at, size in (("z", AT_Z, SIXTEENTH), ("y", AT_Y, QUARTER)):
        pieces = [fresh] + [turn(fresh, along, j) for j in (1, 2, 3)]
        (fresh,) = call(
            functools.partial(join_kernel, at, size), [((2, 4 * size, F), F32)], (s, *pieces)
        )
    other = swap(fresh)
    new_probe = jnp.concatenate(
        [jnp.where(odd, other, fresh), jnp.where(odd, fresh, other)], axis=1
    )

    new_tiles = []
    for i in range(CHUNKS):
        numer = (
            jnp.where(here & (rows[i] >= mine[0]), grads[i], 0.0)
            + jnp.where(there & (rows[i] >= target[0]), moved[i], 0.0)
            + down[i]
        )
        new_tiles.append(tiles[i] + numer / (light[i * R : (i + 1) * R] + 1.0))
    return (jnp.concatenate(new_tiles, axis=1), new_probe)


def solution(mesh):
    in_specs = (P(None, "obj", "pos"), P(), P(("obj", "pos"), None, None), P(("obj", "pos"), None))
    out_specs = (P(None, "obj", "pos"), P())
    return jax.shard_map(body, mesh=mesh, in_specs=in_specs, out_specs=out_specs, check_vma=False)
```

```python
import functools
import math

import jax
import jax.numpy as jnp
import numpy as np
from jax import lax
from jax.experimental import pallas as pl
from jax.experimental.pallas import tpu as pltpu
from jax.sharding import PartitionSpec as P

F = 512
BOUNDS = (0, 192, 352, 512)
SPANS = tuple(zip(BOUNDS[:-1], BOUNDS[1:]))
CHUNKS = len(SPANS)
Y = X = Z = 4
HALF = F // 2
QUARTER, BLOCK = HALF // Z, HALF // Z // Y
F32, BF16 = jnp.float32, jnp.bfloat16
VMEM = pl.BlockSpec(memory_space=pltpu.VMEM)
SMEM = pl.BlockSpec(memory_space=pltpu.SMEM)
ANY = pl.BlockSpec(memory_space=pl.ANY)

ROW, COL, ROW_T, COL_T, CORE, AT_Z, AT_Y, TOUCH = range(8)


def dft_tables():
    idx = np.arange(F)
    angle = (idx[:, None] * idx[None, :] % F) * (2.0 * math.pi / F)
    scale = 1.0 / math.sqrt(F)
    return (
        jnp.asarray((np.cos(angle) * scale).astype(np.float32)).astype(BF16),
        jnp.asarray((-np.sin(angle) * scale).astype(np.float32)).astype(BF16),
    )


def call(kernel, out_shapes, args, after=(), scratch=(), limit=8, space=VMEM, us=0):
    used = len(args)

    def run(*refs):
        kernel(*refs[:used], *refs[used + len(after) :])

    return pl.pallas_call(
        run,
        out_shape=[jax.ShapeDtypeStruct(s, d) for s, d in out_shapes],
        in_specs=[SMEM] + [space] * (used - 1) + [ANY] * len(after),
        out_specs=[VMEM] * len(out_shapes),
        scratch_shapes=list(scratch),
        cost_estimate=pl.CostEstimate(
            flops=1, bytes_accessed=1 + us * 3_500_000, transcendentals=0
        ),
        compiler_params=pltpu.CompilerParams(vmem_limit_bytes=limit * 2**20),
    )(*args, *after)


def iota(shape, dim):
    return lax.broadcasted_iota(jnp.int32, shape, dim)


def back_by(shift):
    return jnp.bitwise_and(F - shift, F - 1)


def prep_kernel(s, wr, wi, probe, col_table, row_table, row_table_t, turned, block):
    r, c = s[ROW], s[COL]
    for k, w in enumerate((wr, wi)):
        w = w[...].astype(F32)
        col_table[k] = pltpu.roll(w, c, 0).astype(BF16)
        row_table[k] = pltpu.roll(w, r, 0).astype(BF16)
        row_table_t[k] = pltpu.roll(w, r, 1).astype(BF16)
        turned[k] = pltpu.roll(pltpu.roll(probe[k], r, 0), c, 1)
    first = s[CORE] * HALF + s[AT_Z] * QUARTER + s[AT_Y] * BLOCK
    block[...] = probe[:, pl.ds(pl.multiple_of(first, BLOCK), BLOCK), :]


def corner(s, which):
    return s[TOUCH + 2 * which], s[TOUCH + 2 * which + 1]


def touch_mask(which, r, c):
    row, col = iota((F, F), 0), iota((F, F), 1)
    inside_rows = row >= r if which < 2 else row < r
    inside_cols = col >= c if which % 2 == 0 else col < c
    return jnp.logical_and(inside_rows, inside_cols)


def probe_light_kernel(s, obj, keep, send):
    value = obj[0] * obj[0] + obj[1] * obj[1]
    total = jnp.zeros((F, F), F32)
    for which in range(4):
        r, c = corner(s, which)
        part = jnp.where(touch_mask(which, r, c), value, 0.0)
        total += pltpu.roll(pltpu.roll(part, back_by(c), 1), back_by(r + s[CORE] * HALF), 0)
    keep[0] = total[:HALF]
    send[0] = total[HALF:]


def light_kernel(s, probe, out):
    power = probe[0] * probe[0] + probe[1] * probe[1]
    total = jnp.zeros((F, F), F32)
    for which in range(4):
        r, c = corner(s, which)
        part = pltpu.roll(pltpu.roll(power, r, 0), c, 1)
        total += jnp.where(touch_mask(which, r, c), part, 0.0)
    out[...] = total


def cut_kernel(s, obj, *refs):
    copies = [
        pltpu.make_async_copy(obj.at[:, first:last], refs[i], refs[CHUNKS].at[i])
        for i, (first, last) in enumerate(SPANS)
    ]
    for copy in copies:
        copy.start()
    for copy in copies:
        copy.wait()


def column_mask(shape, col_at, odd, own):
    col = iota(shape, 1)
    return jnp.logical_xor(col >= col_at, odd if own else jnp.logical_not(odd))


def lend_kernel(span, s, obj, below, out):
    first, last = span
    row = iota((last - first, F), 0) + first
    for k in range(2):
        out[k] = jnp.where(row >= s[ROW_T], obj[k, first:last], below[k])


def half_kernel(span, s, obj, below, beside, turned, table, patch, half):
    first, last = span
    shape = (last - first, F)
    row = iota(shape, 0) + first
    here = column_mask(shape, s[COL], s[CORE] == 1, True)
    m = [
        jnp.where(here, jnp.where(row >= s[ROW], obj[k, first:last], below[k]), beside[k])
        for k in range(2)
    ]
    for k in range(2):
        patch[k] = m[k]
    p_re, p_im = turned[0, first:last], turned[1, first:last]
    psi_re = (p_re * m[0] - p_im * m[1]).astype(BF16)
    psi_im = (p_re * m[1] + p_im * m[0]).astype(BF16)
    psi = jnp.concatenate([psi_re, psi_im], axis=0)
    by_re = jnp.dot(psi, table[0], preferred_element_type=F32)
    by_im = jnp.dot(psi, table[1], preferred_element_type=F32)
    n = last - first
    half[0] = (by_re[:n] - by_im[n:]).astype(BF16)
    half[1] = (by_re[n:] + by_im[:n]).astype(BF16)


def dot_t(a, b):
    return lax.dot_general(a, b, (((1,), (1,)), ((), ())), preferred_element_type=F32)


def fourier_kernel(s, *refs):
    halves, patches = refs[:CHUNKS], refs[CHUNKS : 2 * CHUNKS]
    col_table, row_table, row_table_t, amps, amps_moved = refs[2 * CHUNKS : 2 * CHUNKS + 5]
    err, keep, send, stack, change, back, numer = refs[2 * CHUNKS + 5 :]
    r, c, odd = s[ROW], s[COL], s[CORE] == 1
    for i, (first, last) in enumerate(SPANS):
        for k in range(2):
            stack[first:last, k * F : (k + 1) * F] = halves[i][k]
    wide = 256
    for j in range(0, F, wide):
        at = slice(j, j + wide)
        cols = jnp.concatenate([stack[:, at], stack[:, F + j : F + j + wide]], axis=1)
        by_re = jnp.dot(row_table_t[0], cols, preferred_element_type=F32)
        by_im = jnp.dot(row_table_t[1], cols, preferred_element_type=F32)
        re, im = by_re[:, :wide] - by_im[:, wide:], by_re[:, wide:] + by_im[:, :wide]
        a = jnp.where(odd, amps_moved[0, :, at], amps[0, :, at])
        factor = a / jnp.maximum(jnp.sqrt(re * re + im * im), 0.25) - 1.0
        change[:, :wide] = (factor * re).astype(BF16)
        change[:, wide:] = (factor * im).astype(BF16)
        by_re = jnp.dot(row_table[0], change[...], preferred_element_type=F32)
        by_im = jnp.dot(row_table[1], change[...], preferred_element_type=F32)
        back[0, :, at] = (by_re[:, :wide] + by_im[:, wide:]).astype(BF16)
        back[1, :, at] = (by_re[:, wide:] - by_im[:, :wide]).astype(BF16)
    tall = 128
    for j in range(0, F, tall):
        at = slice(j, j + tall)
        rows = jnp.concatenate([back[0, at], back[1, at]], axis=0)
        by_re, by_im = dot_t(rows, col_table[0]), dot_t(rows, col_table[1])
        re, im = by_re[:tall] + by_im[tall:], by_re[tall:] - by_im[:tall]
        err[0, at] = re
        err[1, at] = im
        for i, (first, last) in enumerate(SPANS):
            low, high = max(first, j), min(last, j + tall)
            if low < high:
                m_re, m_im = (patches[i][k, low - first : high - first] for k in range(2))
                e_re, e_im = re[low - j : high - j], im[low - j : high - j]
                numer[0, low:high] = pltpu.roll(m_re * e_re + m_im * e_im, back_by(c), 1)
                numer[1, low:high] = pltpu.roll(m_re * e_im - m_im * e_re, back_by(c), 1)
    for k in range(2):
        turned_back = pltpu.roll(numer[k], back_by(r + s[CORE] * HALF), 0)
        keep[k] = turned_back[:HALF]
        send[k] = turned_back[HALF:]


def grad_kernel(s, turned, err, grad):
    grad[0] = turned[0] * err[0] + turned[1] * err[1]
    grad[1] = turned[0] * err[1] - turned[1] * err[0]


def fallen_masks(s, below):
    row = iota((F, F), 0)
    odd = s[CORE] == 1
    rows = [row < s[at] if below else row >= s[at] for at in (ROW, ROW_T)]
    here = jnp.logical_and(column_mask((F, F), s[COL], odd, True), rows[0])
    there = jnp.logical_and(column_mask((F, F), s[COL_T], odd, False), rows[1])
    return here, there


def down_kernel(s, grad, moved, down):
    here, there = fallen_masks(s, True)
    for k in range(2):
        down[k] = jnp.where(here, grad[k], 0.0) + jnp.where(there, moved[k], 0.0)


def stay_kernel(s, obj, light, grad, moved, base, scale):
    here, there = fallen_masks(s, False)
    part = 1.0 / (light[...] + 1.0)
    scale[...] = part
    for k in range(2):
        stay = jnp.where(here, grad[k], 0.0) + jnp.where(there, moved[k], 0.0)
        base[k] = obj[k] + stay * part


def object_kernel(s, base, scale, fallen, out):
    for k in range(2):
        out[k] = base[k] + fallen[k] * scale[...]


def turn(value, along, steps):
    if along == "z":
        return lax.ppermute(value, "obj", [(o, (o + 2 * steps) % (2 * Z)) for o in range(2 * Z)])
    pairs = []
    for y in range(Y):
        for x in range(X):
            to = (y, (x + steps) % X) if along == "x" else ((y + steps) % Y, x)
            pairs.append((y * X + x, to[0] * X + to[1]))
    return lax.ppermute(value, "pos", pairs)


def exchange(blocks, along):
    return [blocks[0]] + [turn(blocks[j], along, j) for j in range(1, 4)]


def block_rows(at, j, size):
    return pl.ds(pl.multiple_of(jnp.bitwise_and(at + j, 3) * size, size), size)


def share_kernel(s, numer, numer_got, light, light_got, *outs):
    for j, out in enumerate(outs):
        rows = block_rows(s[AT_Z], j, QUARTER)
        out[:2] = numer[:, rows, :] + numer_got[:, rows, :]
        out[2:] = light[:, rows, :] + light_got[:, rows, :]


def sum_kernel(s, a, b, c, d, *outs):
    for j, out in enumerate(outs):
        rows = block_rows(s[AT_Y], j, BLOCK)
        out[...] = a[:, rows, :] + b[:, rows, :] + c[:, rows, :] + d[:, rows, :]


def add_kernel(s, a, b, c, d, out):
    out[...] = a[...] + b[...] + c[...] + d[...]


def update_kernel(beta, s, a, b, c, d, probe, out):
    total = a[...] + b[...] + c[...] + d[...]
    out[...] = probe[...] + beta * total[:2] / (total[2:3] + 1.0)


def join_kernel(axis, s, *refs):
    for j in range(4):
        refs[4][jnp.bitwise_and(s[axis] - j, 3)] = refs[j][...]


def pair_kernel(s, mine, other, out):
    for ref, half in ((mine, s[CORE]), (other, 1 - s[CORE])):
        for z in range(Z):
            for y in range(Y):
                first = pl.multiple_of(half * HALF + (z * QUARTER + y * BLOCK), BLOCK)
                out[:, pl.ds(first, BLOCK), :] = ref[z, y]


def swap(value):
    return lax.ppermute(value, "obj", [(o, o ^ 1) for o in range(2 * Z)])


def shifted(value, steps):
    n = 2 * Z
    return lax.ppermute(value, "obj", [(o, o + steps) for o in range(n) if 0 <= o + steps < n])


def x_pairs(odd_only=False):
    n = Y * X
    pairs = [(o * n + p, o * n + (p + 1) % n) for o in range(1, 2 * Z, 2) for p in range(n)]
    if not odd_only:
        pairs += [(o * n + p, o * n + p - 1) for o in range(0, 2 * Z, 2) for p in range(1, n)]
    return pairs


def toward(value, odd_only=False):
    return lax.ppermute(value, ("obj", "pos"), x_pairs(odd_only))


def homeward(value):
    return lax.ppermute(value, ("obj", "pos"), [(b, a) for a, b in x_pairs()])


def body(object_field, probe, amplitudes, offsets):
    row_index = lax.axis_index("obj")
    col_index = lax.axis_index("pos")
    core, z, y = row_index % 2, row_index // 2, col_index // X
    place_here = jnp.stack([core, z, y])
    own = offsets[0] - jnp.stack([row_index * F, col_index * F])
    n = Y * X
    left = lax.ppermute(own, "pos", [(p, (p + 1) % n) for p in range(n)])
    above = shifted(jnp.concatenate([own, left]), 1)
    odd = core == 1
    mine, target = jnp.where(odd, left, own), jnp.where(odd, own, left)
    s = jnp.concatenate([mine, target, place_here]).astype(jnp.int32)
    touch = jnp.concatenate([s, own, left, above]).astype(jnp.int32)

    shapes = [((2, last - first, F), F32) for first, last in SPANS]

    tiles = call(
        cut_kernel,
        shapes,
        (own, object_field),
        scratch=[pltpu.SemaphoreType.DMA((CHUNKS,))],
        space=ANY,
    )
    below = [shifted(tile, -1) for tile in tiles]
    amps_moved = toward(amplitudes, odd_only=True)
    lent, beside = [], []

    def lend(i, after):
        lent.extend(
            call(
                functools.partial(lend_kernel, SPANS[i]),
                [shapes[i]],
                (s, object_field, below[i]),
                after=after,
            )
        )
        beside.append(toward(lent[i]))

    lend(0, (amps_moved,))
    lend(1, (lent[0],))
    wr, wi = dft_tables()
    square = ((2, F, F), BF16)
    col_table, row_table, row_table_t, turned, probe_block = call(
        prep_kernel,
        [square] * 3 + [((2, F, F), F32), ((2, BLOCK, F), F32)],
        (s, wr, wi, probe),
        after=(lent[1],),
        limit=16,
    )
    lend(2, (turned,))
    seen, seen_send = call(
        probe_light_kernel,
        [((1, HALF, F), F32)] * 2,
        (touch, object_field),
        after=(lent[2],),
        limit=16,
        us=5,
    )

    patches, halves = [], []
    for i, span in enumerate(SPANS):
        patch, half = call(
            functools.partial(half_kernel, span),
            [shapes[i], (shapes[i][0], BF16)],
            (s, object_field, below[i], beside[i], turned, col_table),
            after=(lent[-1],),
            limit=16,
            us=0 if i == CHUNKS - 1 else 2,
        )
        patches.append(patch)
        halves.append(half)

    err, keep, send = call(
        fourier_kernel,
        [((2, F, F), F32)] + [((2, HALF, F), F32)] * 2,
        (s, *halves, *patches, col_table, row_table, row_table_t, amplitudes, amps_moved),
        after=(seen,),
        limit=24,
        scratch=[
            pltpu.VMEM((F, 2 * F), BF16),
            pltpu.VMEM((F, F), BF16),
            pltpu.VMEM((2, F, F), BF16),
            pltpu.VMEM((2, F, F), F32),
        ],
    )

    (grad,) = call(grad_kernel, [((2, F, F), F32)], (s, turned, err), us=3)
    moved = homeward(grad)
    (light,) = call(light_kernel, [((F, F), F32)], (touch, probe), after=(keep,), limit=16)
    quarter, block = ((3, QUARTER, F), F32), ((3, BLOCK, F), F32)
    parts = call(share_kernel, [quarter] * 4, (s, keep, swap(send), seen, swap(seen_send)))
    parts = call(sum_kernel, [block] * 4, (s, *exchange(parts, "z")), after=(light,))
    (down,) = call(down_kernel, [((2, F, F), F32)], (s, grad, moved), after=(parts[0],))
    fallen = shifted(down, 1)
    (share,) = call(add_kernel, [block], (s, *exchange(parts, "y")), after=(down,))
    beta = 0.5 * math.sqrt(2 * X * Y * Z)
    (fresh,) = call(
        functools.partial(update_kernel, beta),
        [((2, BLOCK, F), F32)],
        (s, *exchange([share] * 4, "x"), probe_block),
    )
    base, scale = call(
        stay_kernel,
        [((2, F, F), F32), ((F, F), F32)],
        (s, object_field, light, grad, moved),
        after=(share,),
    )
    (fresh,) = call(
        functools.partial(join_kernel, AT_Y),
        [((4,) + fresh.shape, F32)],
        (s, *exchange([fresh] * 4, "y")),
        after=(base,),
    )
    (new_object,) = call(object_kernel, [((2, F, F), F32)], (s, base, scale, fallen))
    (fresh,) = call(
        functools.partial(join_kernel, AT_Z),
        [((4,) + fresh.shape, F32)],
        (s, *exchange([fresh] * 4, "z")),
        after=(new_object,),
    )
    (new_probe,) = call(pair_kernel, [((2, F, F), F32)], (s, fresh, swap(fresh)))
    return (new_object, new_probe)


def solution(mesh):
    in_specs = (P(None, "obj", "pos"), P(), P(("obj", "pos"), None, None), P(("obj", "pos"), None))
    out_specs = (P(None, "obj", "pos"), P())
    return jax.shard_map(body, mesh=mesh, in_specs=in_specs, out_specs=out_specs, check_vma=False)
```

```python
import functools
import math

import jax
import jax.numpy as jnp
import numpy as np
from jax import lax
from jax.experimental import pallas as pl
from jax.experimental.pallas import tpu as pltpu
from jax.sharding import PartitionSpec as P

F = 512
BOUNDS = (0, 256, 512)
SPANS = tuple(zip(BOUNDS[:-1], BOUNDS[1:]))
CHUNKS = len(SPANS)
OUT_SPANS = ((0, 256), (256, 512))
Y = X = Z = 4
HALF = F // 2
QUARTER, BLOCK = HALF // Z, HALF // Z // Y
F32, BF16 = jnp.float32, jnp.bfloat16
VMEM = pl.BlockSpec(memory_space=pltpu.VMEM)
SMEM = pl.BlockSpec(memory_space=pltpu.SMEM)
ANY = pl.BlockSpec(memory_space=pl.ANY)

ROW, COL, ROW_T, COL_T, CORE, AT_Z, AT_Y, TOUCH = range(8)


def dft_tables():
    idx = np.arange(F)
    angle = (idx[:, None] * idx[None, :] % F) * (2.0 * math.pi / F)
    scale = 1.0 / math.sqrt(F)
    return (
        jnp.asarray((np.cos(angle) * scale).astype(np.float32)).astype(BF16),
        jnp.asarray((-np.sin(angle) * scale).astype(np.float32)).astype(BF16),
    )


def call(kernel, out_shapes, args, after=(), scratch=(), limit=8, keep=pltpu.VMEM):
    used = len(args)

    def run(*refs):
        kernel(*refs[:used], *refs[used + len(after) :])

    return pl.pallas_call(
        run,
        out_shape=[keep(s, d) for s, d in out_shapes],
        in_specs=[SMEM] + [VMEM] * (used - 1) + [ANY] * len(after),
        out_specs=[VMEM] * len(out_shapes),
        scratch_shapes=list(scratch),
        cost_estimate=pl.CostEstimate(flops=1, bytes_accessed=1, transcendentals=0),
        compiler_params=pltpu.CompilerParams(vmem_limit_bytes=limit * 2**20),
    )(*args, *after)


def iota(shape, dim):
    return lax.broadcasted_iota(jnp.int32, shape, dim)


def back_by(shift):
    return jnp.bitwise_and(F - shift, F - 1)


def prep_kernel(s, wr, wi, probe, col_table, row_table, row_table_t, turned, block):
    r, c = s[ROW], s[COL]
    for k, w in enumerate((wr, wi)):
        w = w[...].astype(F32)
        col_table[k] = pltpu.roll(w, c, 0).astype(BF16)
        row_table[k] = pltpu.roll(w, r, 0).astype(BF16)
        row_table_t[k] = pltpu.roll(w, r, 1).astype(BF16)
        turned[k] = pltpu.roll(pltpu.roll(probe[k], r, 0), c, 1)
    first = s[CORE] * HALF + s[AT_Z] * QUARTER + s[AT_Y] * BLOCK
    block[...] = probe[:, pl.ds(pl.multiple_of(first, BLOCK), BLOCK), :]


def corner(s, which):
    return s[TOUCH + 2 * which], s[TOUCH + 2 * which + 1]


def touch_mask(which, r, c):
    row, col = iota((F, F), 0), iota((F, F), 1)
    inside_rows = row >= r if which < 2 else row < r
    inside_cols = col >= c if which % 2 == 0 else col < c
    return jnp.logical_and(inside_rows, inside_cols)


def probe_light_kernel(s, obj, keep, send):
    value = obj[0] * obj[0] + obj[1] * obj[1]
    total = jnp.zeros((F, F), F32)
    for which in range(4):
        r, c = corner(s, which)
        part = jnp.where(touch_mask(which, r, c), value, 0.0)
        total += pltpu.roll(pltpu.roll(part, back_by(c), 1), back_by(r + s[CORE] * HALF), 0)
    keep[0] = total[:HALF]
    send[0] = total[HALF:]


def light_kernel(s, probe, out):
    power = probe[0] * probe[0] + probe[1] * probe[1]
    total = jnp.zeros((F, F), F32)
    for which in range(4):
        r, c = corner(s, which)
        part = pltpu.roll(pltpu.roll(power, r, 0), c, 1)
        total += jnp.where(touch_mask(which, r, c), part, 0.0)
    out[...] = total


def cut_kernel(obj, *refs):
    copies = [
        pltpu.make_async_copy(obj.at[:, first:last], refs[i], refs[CHUNKS].at[i])
        for i, (first, last) in enumerate(SPANS)
    ]
    for copy in copies:
        copy.start()
    for copy in copies:
        copy.wait()


def cut(obj):
    return pl.pallas_call(
        cut_kernel,
        out_shape=[pltpu.VMEM((2, last - first, F), F32) for first, last in SPANS],
        in_specs=[ANY],
        out_specs=[VMEM] * CHUNKS,
        scratch_shapes=[pltpu.SemaphoreType.DMA((CHUNKS,))],
        cost_estimate=pl.CostEstimate(flops=1, bytes_accessed=1, transcendentals=0),
    )(pltpu.with_memory_space_constraint(obj, pltpu.HBM))


def column_mask(shape, col_at, odd, own):
    col = iota(shape, 1)
    return jnp.logical_xor(col >= col_at, odd if own else jnp.logical_not(odd))


def lend_kernel(span, s, tile, below, out):
    first, last = span
    row = iota((last - first, F), 0) + first
    for k in range(2):
        out[k] = jnp.where(row >= s[ROW_T], tile[k], below[k])


def half_kernel(span, s, tile, below, beside, turned, table, patch, half):
    first, last = span
    shape = (last - first, F)
    row = iota(shape, 0) + first
    here = column_mask(shape, s[COL], s[CORE] == 1, True)
    m = [
        jnp.where(here, jnp.where(row >= s[ROW], tile[k], below[k]), beside[k])
        for k in range(2)
    ]
    for k in range(2):
        patch[k] = m[k]
    p_re, p_im = turned[0, first:last], turned[1, first:last]
    psi_re = (p_re * m[0] - p_im * m[1]).astype(BF16)
    psi_im = (p_re * m[1] + p_im * m[0]).astype(BF16)
    psi = jnp.concatenate([psi_re, psi_im], axis=0)
    by_re = jnp.dot(psi, table[0], preferred_element_type=F32)
    by_im = jnp.dot(psi, table[1], preferred_element_type=F32)
    n = last - first
    half[0] = (by_re[:n] - by_im[n:]).astype(BF16)
    half[1] = (by_re[n:] + by_im[:n]).astype(BF16)


def dot_t(a, b):
    return lax.dot_general(a, b, (((1,), (1,)), ((), ())), preferred_element_type=F32)


def fourier_kernel(s, *refs):
    halves, patches = (refs[i * CHUNKS : (i + 1) * CHUNKS] for i in range(2))
    col_table, row_table, row_table_t, amps, amps_moved, turned = refs[2 * CHUNKS : 2 * CHUNKS + 6]
    grads, (keep, send, stack, change, back, numer) = refs[2 * CHUNKS + 6 :][:2], refs[2 * CHUNKS + 8 :]
    r, c, odd = s[ROW], s[COL], s[CORE] == 1
    for i, (first, last) in enumerate(SPANS):
        for k in range(2):
            stack[first:last, k * F : (k + 1) * F] = halves[i][k]
    wide = 256
    for j in range(0, F, wide):
        at = slice(j, j + wide)
        cols = jnp.concatenate([stack[:, at], stack[:, F + j : F + j + wide]], axis=1)
        by_re = jnp.dot(row_table_t[0], cols, preferred_element_type=F32)
        by_im = jnp.dot(row_table_t[1], cols, preferred_element_type=F32)
        re, im = by_re[:, :wide] - by_im[:, wide:], by_re[:, wide:] + by_im[:, :wide]
        a = jnp.where(odd, amps_moved[0, :, at], amps[0, :, at])
        factor = a / jnp.maximum(jnp.sqrt(re * re + im * im), 0.25) - 1.0
        change[:, :wide] = (factor * re).astype(BF16)
        change[:, wide:] = (factor * im).astype(BF16)
        by_re = jnp.dot(row_table[0], change[...], preferred_element_type=F32)
        by_im = jnp.dot(row_table[1], change[...], preferred_element_type=F32)
        back[0, :, at] = (by_re[:, :wide] + by_im[:, wide:]).astype(BF16)
        back[1, :, at] = (by_re[:, wide:] - by_im[:, :wide]).astype(BF16)
    tall = 128
    for j in range(0, F, tall):
        at = slice(j, j + tall)
        rows = jnp.concatenate([back[0, at], back[1, at]], axis=0)
        by_re, by_im = dot_t(rows, col_table[0]), dot_t(rows, col_table[1])
        re, im = by_re[:tall] + by_im[tall:], by_re[tall:] - by_im[:tall]
        p_re, p_im = turned[0, at], turned[1, at]
        grad, rows = next((g, slice(j - a, j - a + tall)) for g, (a, b) in zip(grads, OUT_SPANS) if j < b)
        grad[0, rows] = p_re * re + p_im * im
        grad[1, rows] = p_re * im - p_im * re
        for i, (first, last) in enumerate(SPANS):
            low, high = max(first, j), min(last, j + tall)
            if low < high:
                m_re, m_im = (patches[i][k, low - first : high - first] for k in range(2))
                e_re, e_im = re[low - j : high - j], im[low - j : high - j]
                numer[0, low:high] = pltpu.roll(m_re * e_re + m_im * e_im, back_by(c), 1)
                numer[1, low:high] = pltpu.roll(m_re * e_im - m_im * e_re, back_by(c), 1)
    for k in range(2):
        turned_back = pltpu.roll(numer[k], back_by(r + s[CORE] * HALF), 0)
        keep[k] = turned_back[:HALF]
        send[k] = turned_back[HALF:]


def fallen_masks(span, s, below):
    shape = (span[1] - span[0], F)
    row = iota(shape, 0) + span[0]
    odd = s[CORE] == 1
    rows = [row < s[at] if below else row >= s[at] for at in (ROW, ROW_T)]
    here = jnp.logical_and(column_mask(shape, s[COL], odd, True), rows[0])
    there = jnp.logical_and(column_mask(shape, s[COL_T], odd, False), rows[1])
    return here, there


def down_kernel(span, s, grad, moved, down):
    here, there = fallen_masks(span, s, True)
    for k in range(2):
        down[k] = jnp.where(here, grad[k], 0.0) + jnp.where(there, moved[k], 0.0)


def stay_kernel(s, obj, light, *refs):
    grads, moved, (base, scale) = refs[:2], refs[2:4], refs[4:]
    for i, span in enumerate(OUT_SPANS):
        at = slice(*span)
        here, there = fallen_masks(span, s, False)
        part = 1.0 / (light[at] + 1.0)
        scale[at] = part
        for k in range(2):
            stay = jnp.where(here, grads[i][k], 0.0) + jnp.where(there, moved[i][k], 0.0)
            base[k, at] = obj[k, at] + stay * part


def object_kernel(s, base, scale, *refs):
    fallen, (out, ready) = refs[:2], refs[2:]
    ready[...] = jnp.zeros(ready.shape, F32)
    for i, span in enumerate(OUT_SPANS):
        at = slice(*span)
        for k in range(2):
            out[k, at] = base[k, at] + fallen[i][k] * scale[at]


def turn(value, along, steps):
    if along == "z":
        return lax.ppermute(value, "obj", [(o, (o + 2 * steps) % (2 * Z)) for o in range(2 * Z)])
    pairs = []
    for y in range(Y):
        for x in range(X):
            to = (y, (x + steps) % X) if along == "x" else ((y + steps) % Y, x)
            pairs.append((y * X + x, to[0] * X + to[1]))
    return lax.ppermute(value, "pos", pairs)


def exchange(blocks, along):
    return [blocks[0]] + [turn(blocks[j], along, j) for j in range(1, 4)]


def block_rows(at, j, size):
    return pl.ds(pl.multiple_of(jnp.bitwise_and(at + j, 3) * size, size), size)


def share_kernel(s, keep, got, *outs):
    for j, out in enumerate(outs):
        rows = block_rows(s[AT_Z], j, QUARTER)
        out[...] = keep[:, rows, :] + got[:, rows, :]


def sum_kernel(s, *refs):
    numer, light, outs = refs[:4], refs[4:8], refs[8:]
    for j, out in enumerate(outs):
        rows = block_rows(s[AT_Y], j, BLOCK)
        for first, parts in ((0, numer), (2, light)):
            a, b, c, d = [ref[:, rows, :] for ref in parts]
            out[first : first + a.shape[0]] = a + b + c + d


def add_kernel(s, a, b, c, d, out):
    out[...] = a[...] + b[...] + c[...] + d[...]


def update_kernel(beta, s, a, b, c, d, probe, out):
    total = a[...] + b[...] + c[...] + d[...]
    out[...] = probe[...] + beta * total[:2] / (total[2:3] + 1.0)


def join_kernel(axis, s, *refs):
    for j in range(4):
        refs[4][jnp.bitwise_and(s[axis] - j, 3)] = refs[j][...]


def pair_kernel(s, mine, other, out):
    for ref, half in ((mine, s[CORE]), (other, 1 - s[CORE])):
        for z in range(Z):
            for y in range(Y):
                first = pl.multiple_of(half * HALF + (z * QUARTER + y * BLOCK), BLOCK)
                out[:, pl.ds(first, BLOCK), :] = ref[z, y]


def swap(value):
    return lax.ppermute(value, "obj", [(o, o ^ 1) for o in range(2 * Z)])


def shifted(value, steps):
    n = 2 * Z
    return lax.ppermute(value, "obj", [(o, o + steps) for o in range(n) if 0 <= o + steps < n])


def x_pairs(odd_only=False):
    n = Y * X
    pairs = [(o * n + p, o * n + (p + 1) % n) for o in range(1, 2 * Z, 2) for p in range(n)]
    if not odd_only:
        pairs += [(o * n + p, o * n + p - 1) for o in range(0, 2 * Z, 2) for p in range(1, n)]
    return pairs


def toward(value, odd_only=False):
    return lax.ppermute(value, ("obj", "pos"), x_pairs(odd_only))


def homeward(value):
    return lax.ppermute(value, ("obj", "pos"), [(b, a) for a, b in x_pairs()])


def body(object_field, probe, amplitudes, offsets):
    row_index = lax.axis_index("obj")
    col_index = lax.axis_index("pos")
    core, z, y = row_index % 2, row_index // 2, col_index // X
    place_here = jnp.stack([core, z, y])
    own = offsets[0] - jnp.stack([row_index * F, col_index * F])
    n = Y * X
    left = lax.ppermute(own, "pos", [(p, (p + 1) % n) for p in range(n)])
    above = shifted(jnp.concatenate([own, left]), 1)
    odd = core == 1
    mine, target = jnp.where(odd, left, own), jnp.where(odd, own, left)
    s = jnp.concatenate([mine, target, place_here]).astype(jnp.int32)
    touch = jnp.concatenate([s, own, left, above]).astype(jnp.int32)

    shapes = [((2, last - first, F), F32) for first, last in SPANS]

    tiles = cut(object_field)
    below = [shifted(tile, -1) for tile in tiles]
    amps_moved = toward(amplitudes, odd_only=True)
    lent, beside = [], []

    def lend(i, after):
        lent.extend(
            call(
                functools.partial(lend_kernel, SPANS[i]),
                [shapes[i]],
                (s, tiles[i], below[i]),
                after=after,
                keep=jax.ShapeDtypeStruct,
            )
        )
        beside.append(toward(lent[i]))

    lend(0, (amps_moved,))
    seen, seen_send = call(
        probe_light_kernel,
        [((1, HALF, F), F32)] * 2,
        (touch, object_field),
        after=(lent[0],),
        limit=16,
    )
    lend(1, (seen,))
    wr, wi = dft_tables()
    square = ((2, F, F), BF16)
    col_table, row_table, row_table_t, turned, probe_block = call(
        prep_kernel,
        [square] * 3 + [((2, F, F), F32), ((2, BLOCK, F), F32)],
        (s, wr, wi, probe),
        after=(lent[1],),
        limit=16,
        keep=jax.ShapeDtypeStruct,
    )
    seen = call(
        share_kernel, [((1, QUARTER, F), F32)] * 4, (s, seen, swap(seen_send)), after=(turned,)
    )
    seen = exchange(seen, "z")

    patches, halves = [], []
    for i, span in enumerate(SPANS):
        patch, half = call(
            functools.partial(half_kernel, span),
            [shapes[i], (shapes[i][0], BF16)],
            (s, tiles[i], below[i], beside[i], turned, col_table),
            after=(seen[0],) if i == 0 else (patches[-1], *seen),
            limit=16,
            keep=jax.ShapeDtypeStruct,
        )
        patches.append(patch)
        halves.append(half)

    half_tile = ((2, HALF, F), F32)
    *grads, keep, send = call(
        fourier_kernel,
        [half_tile] * 2 + [((2, HALF, F), F32)] * 2,
        (s, *halves, *patches, col_table, row_table, row_table_t, amplitudes, amps_moved, turned),
        limit=24,
        scratch=[
            pltpu.VMEM((F, 2 * F), BF16),
            pltpu.VMEM((F, F), BF16),
            pltpu.VMEM((2, F, F), BF16),
            pltpu.VMEM((2, F, F), F32),
        ],
    )

    quarter, block = ((2, QUARTER, F), F32), ((3, BLOCK, F), F32)
    parts = call(share_kernel, [quarter] * 4, (s, keep, swap(send)))
    moved = [homeward(grad) for grad in grads]
    (light,) = call(light_kernel, [((F, F), F32)], (touch, probe), after=(parts[0],), limit=16)
    (down,) = call(
        functools.partial(down_kernel, OUT_SPANS[0]), [half_tile], (s, grads[0], moved[0]), after=(light,)
    )
    fallen = [shifted(down, 1)]
    parts = call(sum_kernel, [block] * 4, (s, *exchange(parts, "z"), *seen), after=(down,))
    parts = exchange(parts, "y")
    (down,) = call(
        functools.partial(down_kernel, OUT_SPANS[1]), [half_tile], (s, grads[1], moved[1]), after=parts
    )
    fallen.append(shifted(down, 1))
    (share,) = call(add_kernel, [block], (s, *parts))
    beta = 0.5 * math.sqrt(2 * X * Y * Z)
    (fresh,) = call(
        functools.partial(update_kernel, beta),
        [((2, BLOCK, F), F32)],
        (s, *exchange([share] * 4, "x"), probe_block),
        after=(down,),
    )
    base, scale = call(
        stay_kernel,
        [((2, F, F), F32), ((F, F), F32)],
        (s, object_field, light, *grads, *moved),
        after=(share,),
    )
    (fresh,) = call(
        functools.partial(join_kernel, AT_Y),
        [((4,) + fresh.shape, F32)],
        (s, *exchange([fresh] * 4, "y")),
        after=(base,),
    )
    new_object, ready = call(
        object_kernel, [((2, F, F), F32), ((8, 128), F32)], (s, base, scale, *fallen), keep=pltpu.HBM
    )
    (fresh,) = call(
        functools.partial(join_kernel, AT_Z),
        [((4,) + fresh.shape, F32)],
        (s, *exchange([fresh] * 4, "z")),
        after=(ready,),
    )
    (new_probe,) = call(pair_kernel, [((2, F, F), F32)], (s, fresh, swap(fresh)), keep=pltpu.HBM)
    return (new_object, new_probe)


def solution(mesh):
    in_specs = (P(None, "obj", "pos"), P(), P(("obj", "pos"), None, None), P(("obj", "pos"), None))
    out_specs = (P(None, "obj", "pos"), P())
    return jax.shard_map(body, mesh=mesh, in_specs=in_specs, out_specs=out_specs, check_vma=False)
```

```python
import functools
import math

import jax
import jax.numpy as jnp
import numpy as np
from jax import lax
from jax.experimental import pallas as pl
from jax.experimental.pallas import tpu as pltpu
from jax.sharding import PartitionSpec as P

F = 512
BOUNDS = (0, 256, 512)
SPANS = tuple(zip(BOUNDS[:-1], BOUNDS[1:]))
CHUNKS = len(SPANS)
OUT_SPANS = ((0, 256), (256, 512))
Y = X = Z = 4
HALF = F // 2
QUARTER, BLOCK = HALF // Z, HALF // Z // Y
F32, BF16 = jnp.float32, jnp.bfloat16
VMEM = pl.BlockSpec(memory_space=pltpu.VMEM)
SMEM = pl.BlockSpec(memory_space=pltpu.SMEM)
ANY = pl.BlockSpec(memory_space=pl.ANY)

ROW, COL, ROW_T, COL_T, CORE, AT_Z, AT_Y, TOUCH = range(8)


def dft_tables():
    idx = np.arange(F)
    angle = (idx[:, None] * idx[None, :] % F) * (2.0 * math.pi / F)
    scale = 1.0 / math.sqrt(F)
    return (
        jnp.asarray((np.cos(angle) * scale).astype(np.float32)).astype(BF16),
        jnp.asarray((-np.sin(angle) * scale).astype(np.float32)).astype(BF16),
    )


def call(kernel, out_shapes, args, after=(), scratch=(), limit=8, keep=pltpu.VMEM):
    used = len(args)

    def run(*refs):
        kernel(*refs[:used], *refs[used + len(after) :])

    return pl.pallas_call(
        run,
        out_shape=[keep(s, d) for s, d in out_shapes],
        in_specs=[SMEM] + [VMEM] * (used - 1) + [ANY] * len(after),
        out_specs=[VMEM] * len(out_shapes),
        scratch_shapes=list(scratch),
        cost_estimate=pl.CostEstimate(flops=1, bytes_accessed=1, transcendentals=0),
        compiler_params=pltpu.CompilerParams(vmem_limit_bytes=limit * 2**20),
    )(*args, *after)


def iota(shape, dim):
    return lax.broadcasted_iota(jnp.int32, shape, dim)


def back_by(shift):
    return jnp.bitwise_and(F - shift, F - 1)


def prep_kernel(s, wr, wi, probe, col_table, row_table, row_table_t, turned, block):
    r, c = s[ROW], s[COL]
    for k, w in enumerate((wr, wi)):
        w = w[...].astype(F32)
        col_table[k] = pltpu.roll(w, c, 0).astype(BF16)
        row_table[k] = pltpu.roll(w, r, 0).astype(BF16)
        row_table_t[k] = pltpu.roll(w, r, 1).astype(BF16)
        turned[k] = pltpu.roll(pltpu.roll(probe[k], r, 0), c, 1)
    first = s[CORE] * HALF + s[AT_Z] * QUARTER + s[AT_Y] * BLOCK
    block[...] = probe[:, pl.ds(pl.multiple_of(first, BLOCK), BLOCK), :]


def corner(s, which):
    return s[TOUCH + 2 * which], s[TOUCH + 2 * which + 1]


def touch_mask(which, r, c):
    row, col = iota((F, F), 0), iota((F, F), 1)
    inside_rows = row >= r if which < 2 else row < r
    inside_cols = col >= c if which % 2 == 0 else col < c
    return jnp.logical_and(inside_rows, inside_cols)


def probe_light_kernel(s, obj, keep, send):
    value = obj[0] * obj[0] + obj[1] * obj[1]
    total = jnp.zeros((F, F), F32)
    for which in range(4):
        r, c = corner(s, which)
        part = jnp.where(touch_mask(which, r, c), value, 0.0)
        total += pltpu.roll(pltpu.roll(part, back_by(c), 1), back_by(r + s[CORE] * HALF), 0)
    keep[0] = total[:HALF]
    send[0] = total[HALF:]


def light_kernel(s, probe, out):
    power = probe[0] * probe[0] + probe[1] * probe[1]
    total = jnp.zeros((F, F), F32)
    for which in range(4):
        r, c = corner(s, which)
        part = pltpu.roll(pltpu.roll(power, r, 0), c, 1)
        total += jnp.where(touch_mask(which, r, c), part, 0.0)
    out[...] = total


def cut(obj, span, after=()):
    def kernel(obj, *refs):
        copy = pltpu.make_async_copy(obj.at[:, span[0] : span[1]], refs[-2], refs[-1])
        copy.start()
        copy.wait()

    return pl.pallas_call(
        kernel,
        out_shape=pltpu.VMEM((2, span[1] - span[0], F), F32),
        in_specs=[ANY] * (1 + len(after)),
        out_specs=VMEM,
        scratch_shapes=[pltpu.SemaphoreType.DMA],
        cost_estimate=pl.CostEstimate(flops=1, bytes_accessed=1, transcendentals=0),
    )(pltpu.with_memory_space_constraint(obj, pltpu.HBM), *after)


def column_mask(shape, col_at, odd, own):
    col = iota(shape, 1)
    return jnp.logical_xor(col >= col_at, odd if own else jnp.logical_not(odd))


def lend_kernel(span, s, tile, below, out):
    first, last = span
    row = iota((last - first, F), 0) + first
    for k in range(2):
        out[k] = jnp.where(row >= s[ROW_T], tile[k], below[k])


def half_kernel(span, s, tile, below, beside, turned, table, patch, half):
    first, last = span
    shape = (last - first, F)
    row = iota(shape, 0) + first
    here = column_mask(shape, s[COL], s[CORE] == 1, True)
    m = [
        jnp.where(here, jnp.where(row >= s[ROW], tile[k], below[k]), beside[k])
        for k in range(2)
    ]
    for k in range(2):
        patch[k] = m[k]
    p_re, p_im = turned[0, first:last], turned[1, first:last]
    psi_re = (p_re * m[0] - p_im * m[1]).astype(BF16)
    psi_im = (p_re * m[1] + p_im * m[0]).astype(BF16)
    psi = jnp.concatenate([psi_re, psi_im], axis=0)
    by_re = jnp.dot(psi, table[0], preferred_element_type=F32)
    by_im = jnp.dot(psi, table[1], preferred_element_type=F32)
    n = last - first
    half[0] = (by_re[:n] - by_im[n:]).astype(BF16)
    half[1] = (by_re[n:] + by_im[:n]).astype(BF16)


def dot_t(a, b):
    return lax.dot_general(a, b, (((1,), (1,)), ((), ())), preferred_element_type=F32)


def fourier_kernel(s, *refs):
    halves, patches = (refs[i * CHUNKS : (i + 1) * CHUNKS] for i in range(2))
    col_table, row_table, row_table_t, amps, amps_moved, turned = refs[2 * CHUNKS : 2 * CHUNKS + 6]
    grads, (keep, send, stack, change, back, numer) = refs[2 * CHUNKS + 6 :][:2], refs[2 * CHUNKS + 8 :]
    r, c, odd = s[ROW], s[COL], s[CORE] == 1
    for i, (first, last) in enumerate(SPANS):
        for k in range(2):
            stack[first:last, k * F : (k + 1) * F] = halves[i][k]
    wide = 256
    for j in range(0, F, wide):
        at = slice(j, j + wide)
        cols = jnp.concatenate([stack[:, at], stack[:, F + j : F + j + wide]], axis=1)
        by_re = jnp.dot(row_table_t[0], cols, preferred_element_type=F32)
        by_im = jnp.dot(row_table_t[1], cols, preferred_element_type=F32)
        re, im = by_re[:, :wide] - by_im[:, wide:], by_re[:, wide:] + by_im[:, :wide]
        a = jnp.where(odd, amps_moved[0, :, at], amps[0, :, at])
        factor = a / jnp.maximum(jnp.sqrt(re * re + im * im), 0.25) - 1.0
        change[:, :wide] = (factor * re).astype(BF16)
        change[:, wide:] = (factor * im).astype(BF16)
        by_re = jnp.dot(row_table[0], change[...], preferred_element_type=F32)
        by_im = jnp.dot(row_table[1], change[...], preferred_element_type=F32)
        back[0, :, at] = (by_re[:, :wide] + by_im[:, wide:]).astype(BF16)
        back[1, :, at] = (by_re[:, wide:] - by_im[:, :wide]).astype(BF16)
    tall = 128
    for j in range(0, F, tall):
        at = slice(j, j + tall)
        rows = jnp.concatenate([back[0, at], back[1, at]], axis=0)
        by_re, by_im = dot_t(rows, col_table[0]), dot_t(rows, col_table[1])
        re, im = by_re[:tall] + by_im[tall:], by_re[tall:] - by_im[:tall]
        p_re, p_im = turned[0, at], turned[1, at]
        grad, rows = next((g, slice(j - a, j - a + tall)) for g, (a, b) in zip(grads, OUT_SPANS) if j < b)
        grad[0, rows] = p_re * re + p_im * im
        grad[1, rows] = p_re * im - p_im * re
        for i, (first, last) in enumerate(SPANS):
            low, high = max(first, j), min(last, j + tall)
            if low < high:
                m_re, m_im = (patches[i][k, low - first : high - first] for k in range(2))
                e_re, e_im = re[low - j : high - j], im[low - j : high - j]
                numer[0, low:high] = pltpu.roll(m_re * e_re + m_im * e_im, back_by(c), 1)
                numer[1, low:high] = pltpu.roll(m_re * e_im - m_im * e_re, back_by(c), 1)
    for k in range(2):
        turned_back = pltpu.roll(numer[k], back_by(r + s[CORE] * HALF), 0)
        keep[k] = turned_back[:HALF]
        send[k] = turned_back[HALF:]


def fallen_masks(span, s, below):
    shape = (span[1] - span[0], F)
    row = iota(shape, 0) + span[0]
    odd = s[CORE] == 1
    rows = [row < s[at] if below else row >= s[at] for at in (ROW, ROW_T)]
    here = jnp.logical_and(column_mask(shape, s[COL], odd, True), rows[0])
    there = jnp.logical_and(column_mask(shape, s[COL_T], odd, False), rows[1])
    return here, there


def down_kernel(span, s, grad, moved, down):
    here, there = fallen_masks(span, s, True)
    for k in range(2):
        down[k] = jnp.where(here, grad[k], 0.0) + jnp.where(there, moved[k], 0.0)


def stay_kernel(s, obj, light, *refs):
    grads, moved, (base, scale) = refs[:2], refs[2:4], refs[4:]
    for i, span in enumerate(OUT_SPANS):
        at = slice(*span)
        here, there = fallen_masks(span, s, False)
        part = 1.0 / (light[at] + 1.0)
        scale[at] = part
        for k in range(2):
            stay = jnp.where(here, grads[i][k], 0.0) + jnp.where(there, moved[i][k], 0.0)
            base[k, at] = obj[k, at] + stay * part


def object_kernel(s, base, scale, *refs):
    fallen, (out, ready) = refs[:2], refs[2:]
    ready[...] = jnp.zeros(ready.shape, F32)
    for i, span in enumerate(OUT_SPANS):
        at = slice(*span)
        for k in range(2):
            out[k, at] = base[k, at] + fallen[i][k] * scale[at]


def turn(value, along, steps):
    if along == "z":
        return lax.ppermute(value, "obj", [(o, (o + 2 * steps) % (2 * Z)) for o in range(2 * Z)])
    pairs = []
    for y in range(Y):
        for x in range(X):
            to = (y, (x + steps) % X) if along == "x" else ((y + steps) % Y, x)
            pairs.append((y * X + x, to[0] * X + to[1]))
    return lax.ppermute(value, "pos", pairs)


def exchange(blocks, along):
    return [blocks[0]] + [turn(blocks[j], along, j) for j in range(1, 4)]


def block_rows(at, j, size):
    return pl.ds(pl.multiple_of(jnp.bitwise_and(at + j, 3) * size, size), size)


def share_kernel(s, keep, got, *outs):
    for j, out in enumerate(outs):
        rows = block_rows(s[AT_Z], j, QUARTER)
        out[...] = keep[:, rows, :] + got[:, rows, :]


def sum_kernel(s, *refs):
    numer, light, outs = refs[:4], refs[4:8], refs[8:]
    for j, out in enumerate(outs):
        rows = block_rows(s[AT_Y], j, BLOCK)
        for first, parts in ((0, numer), (2, light)):
            a, b, c, d = [ref[:, rows, :] for ref in parts]
            out[first : first + a.shape[0]] = a + b + c + d


def add_kernel(s, a, b, c, d, out):
    out[...] = a[...] + b[...] + c[...] + d[...]


def update_kernel(beta, s, a, b, c, d, probe, out):
    total = a[...] + b[...] + c[...] + d[...]
    out[...] = probe[...] + beta * total[:2] / (total[2:3] + 1.0)


def join_kernel(axis, s, *refs):
    for j in range(4):
        refs[4][jnp.bitwise_and(s[axis] - j, 3)] = refs[j][...]


def pair_kernel(s, mine, other, out):
    for ref, half in ((mine, s[CORE]), (other, 1 - s[CORE])):
        for z in range(Z):
            for y in range(Y):
                first = pl.multiple_of(half * HALF + (z * QUARTER + y * BLOCK), BLOCK)
                out[:, pl.ds(first, BLOCK), :] = ref[z, y]


def swap(value):
    return lax.ppermute(value, "obj", [(o, o ^ 1) for o in range(2 * Z)])


def shifted(value, steps):
    n = 2 * Z
    return lax.ppermute(value, "obj", [(o, o + steps) for o in range(n) if 0 <= o + steps < n])


def x_pairs(odd_only=False):
    n = Y * X
    pairs = [(o * n + p, o * n + (p + 1) % n) for o in range(1, 2 * Z, 2) for p in range(n)]
    if not odd_only:
        pairs += [(o * n + p, o * n + p - 1) for o in range(0, 2 * Z, 2) for p in range(1, n)]
    return pairs


def toward(value, odd_only=False):
    return lax.ppermute(value, ("obj", "pos"), x_pairs(odd_only))


def homeward(value):
    return lax.ppermute(value, ("obj", "pos"), [(b, a) for a, b in x_pairs()])


def body(object_field, probe, amplitudes, offsets):
    row_index = lax.axis_index("obj")
    col_index = lax.axis_index("pos")
    core, z, y = row_index % 2, row_index // 2, col_index // X
    place_here = jnp.stack([core, z, y])
    own = offsets[0] - jnp.stack([row_index * F, col_index * F])
    n = Y * X
    left = lax.ppermute(own, "pos", [(p, (p + 1) % n) for p in range(n)])
    above = shifted(jnp.concatenate([own, left]), 1)
    odd = core == 1
    mine, target = jnp.where(odd, left, own), jnp.where(odd, own, left)
    s = jnp.concatenate([mine, target, place_here]).astype(jnp.int32)
    touch = jnp.concatenate([s, own, left, above]).astype(jnp.int32)

    shapes = [((2, last - first, F), F32) for first, last in SPANS]

    tiles = [cut(object_field, SPANS[0]), cut(object_field, SPANS[1], (left,))]
    below = [shifted(tile, -1) for tile in tiles]
    amps_moved = toward(amplitudes, odd_only=True)
    lent, beside = [], []

    def lend(i, after):
        lent.extend(
            call(
                functools.partial(lend_kernel, SPANS[i]),
                [shapes[i]],
                (s, tiles[i], below[i]),
                after=after,
                keep=jax.ShapeDtypeStruct,
            )
        )
        beside.append(toward(lent[i]))

    lend(0, ())
    seen, seen_send = call(
        probe_light_kernel,
        [((1, HALF, F), F32)] * 2,
        (touch, object_field),
        after=(lent[0], amps_moved),
        limit=16,
    )
    lend(1, (seen,))
    wr, wi = dft_tables()
    square = ((2, F, F), BF16)
    col_table, row_table, row_table_t, turned, probe_block = call(
        prep_kernel,
        [square] * 3 + [((2, F, F), F32), ((2, BLOCK, F), F32)],
        (s, wr, wi, probe),
        after=(lent[1],),
        limit=16,
        keep=jax.ShapeDtypeStruct,
    )
    seen = call(
        share_kernel, [((1, QUARTER, F), F32)] * 4, (s, seen, swap(seen_send)), after=(turned,)
    )
    seen = exchange(seen, "z")

    patches, halves = [], []
    for i, span in enumerate(SPANS):
        patch, half = call(
            functools.partial(half_kernel, span),
            [shapes[i], (shapes[i][0], BF16)],
            (s, tiles[i], below[i], beside[i], turned, col_table),
            after=(seen[0],) if i == 0 else (patches[-1], *seen),
            limit=16,
            keep=jax.ShapeDtypeStruct,
        )
        patches.append(patch)
        halves.append(half)

    half_tile = ((2, HALF, F), F32)
    *grads, keep, send = call(
        fourier_kernel,
        [half_tile] * 2 + [((2, HALF, F), F32)] * 2,
        (s, *halves, *patches, col_table, row_table, row_table_t, amplitudes, amps_moved, turned),
        limit=24,
        scratch=[
            pltpu.VMEM((F, 2 * F), BF16),
            pltpu.VMEM((F, F), BF16),
            pltpu.VMEM((2, F, F), BF16),
            pltpu.VMEM((2, F, F), F32),
        ],
    )

    quarter, block = ((2, QUARTER, F), F32), ((3, BLOCK, F), F32)
    parts = call(share_kernel, [quarter] * 4, (s, keep, swap(send)))
    moved = [homeward(grad) for grad in grads]
    (light,) = call(light_kernel, [((F, F), F32)], (touch, probe), after=(parts[0],), limit=16)
    (down,) = call(
        functools.partial(down_kernel, OUT_SPANS[0]), [half_tile], (s, grads[0], moved[0]), after=(light,)
    )
    fallen = [shifted(down, 1)]
    parts = call(sum_kernel, [block] * 4, (s, *exchange(parts, "z"), *seen), after=(down,))
    parts = exchange(parts, "y")
    (down,) = call(
        functools.partial(down_kernel, OUT_SPANS[1]), [half_tile], (s, grads[1], moved[1]), after=parts
    )
    fallen.append(shifted(down, 1))
    (share,) = call(add_kernel, [block], (s, *parts))
    beta = 0.5 * math.sqrt(2 * X * Y * Z)
    (fresh,) = call(
        functools.partial(update_kernel, beta),
        [((2, BLOCK, F), F32)],
        (s, *exchange([share] * 4, "x"), probe_block),
        after=(down,),
    )
    base, scale = call(
        stay_kernel,
        [((2, F, F), F32), ((F, F), F32)],
        (s, object_field, light, *grads, *moved),
        after=(share,),
    )
    (fresh,) = call(
        functools.partial(join_kernel, AT_Y),
        [((4,) + fresh.shape, F32)],
        (s, *exchange([fresh] * 4, "y")),
        after=(base,),
    )
    new_object, ready = call(
        object_kernel, [((2, F, F), F32), ((8, 128), F32)], (s, base, scale, *fallen), keep=pltpu.HBM
    )
    (fresh,) = call(
        functools.partial(join_kernel, AT_Z),
        [((4,) + fresh.shape, F32)],
        (s, *exchange([fresh] * 4, "z")),
        after=(ready,),
    )
    (new_probe,) = call(pair_kernel, [((2, F, F), F32)], (s, fresh, swap(fresh)), keep=pltpu.HBM)
    return (new_object, new_probe)


def solution(mesh):
    in_specs = (P(None, "obj", "pos"), P(), P(("obj", "pos"), None, None), P(("obj", "pos"), None))
    out_specs = (P(None, "obj", "pos"), P())
    return jax.shard_map(body, mesh=mesh, in_specs=in_specs, out_specs=out_specs, check_vma=False)
```

```python
import functools
import math

import jax
import jax.numpy as jnp
import numpy as np
from jax import lax
from jax.experimental import pallas as pl
from jax.experimental.pallas import tpu as pltpu
from jax.sharding import PartitionSpec as P

F = 512
BOUNDS = (0, 256, 512)
SPANS = tuple(zip(BOUNDS[:-1], BOUNDS[1:]))
CHUNKS = len(SPANS)
OUT_SPANS = ((0, 256), (256, 512))
Y = X = Z = 4
HALF = F // 2
QUARTER, BLOCK = HALF // Z, HALF // Z // Y
F32, BF16 = jnp.float32, jnp.bfloat16
VMEM = pl.BlockSpec(memory_space=pltpu.VMEM)
SMEM = pl.BlockSpec(memory_space=pltpu.SMEM)
ANY = pl.BlockSpec(memory_space=pl.ANY)

ROW, COL, ROW_T, COL_T, CORE, AT_Z, AT_Y, TOUCH = range(8)


def dft_tables():
    idx = np.arange(F)
    angle = (idx[:, None] * idx[None, :] % F) * (2.0 * math.pi / F)
    scale = 1.0 / math.sqrt(F)
    return (
        jnp.asarray((np.cos(angle) * scale).astype(np.float32)).astype(BF16),
        jnp.asarray((-np.sin(angle) * scale).astype(np.float32)).astype(BF16),
    )


def call(kernel, out_shapes, args, after=(), scratch=(), limit=8, keep=pltpu.VMEM):
    used = len(args)

    def run(*refs):
        kernel(*refs[:used], *refs[used + len(after) :])

    return pl.pallas_call(
        run,
        out_shape=[keep(s, d) for s, d in out_shapes],
        in_specs=[SMEM] + [VMEM] * (used - 1) + [ANY] * len(after),
        out_specs=[VMEM] * len(out_shapes),
        scratch_shapes=list(scratch),
        cost_estimate=pl.CostEstimate(flops=1, bytes_accessed=1, transcendentals=0),
        compiler_params=pltpu.CompilerParams(vmem_limit_bytes=limit * 2**20),
    )(*args, *after)


def iota(shape, dim):
    return lax.broadcasted_iota(jnp.int32, shape, dim)


def back_by(shift):
    return jnp.bitwise_and(F - shift, F - 1)


def prep_kernel(s, wr, wi, probe, col_table, row_table, row_table_t, turned, block):
    r, c = s[ROW], s[COL]
    for k, w in enumerate((wr, wi)):
        w = w[...].astype(F32)
        col_table[k] = pltpu.roll(w, c, 0).astype(BF16)
        row_table[k] = pltpu.roll(w, r, 0).astype(BF16)
        row_table_t[k] = pltpu.roll(w, r, 1).astype(BF16)
        turned[k] = pltpu.roll(pltpu.roll(probe[k], r, 0), c, 1)
    first = s[CORE] * HALF + s[AT_Z] * QUARTER + s[AT_Y] * BLOCK
    block[...] = probe[:, pl.ds(pl.multiple_of(first, BLOCK), BLOCK), :]


def corner(s, which):
    return s[TOUCH + 2 * which], s[TOUCH + 2 * which + 1]


def touch_mask(which, r, c):
    row, col = iota((F, F), 0), iota((F, F), 1)
    inside_rows = row >= r if which < 2 else row < r
    inside_cols = col >= c if which % 2 == 0 else col < c
    return jnp.logical_and(inside_rows, inside_cols)


def probe_light_kernel(s, obj, keep, send):
    value = obj[0] * obj[0] + obj[1] * obj[1]
    total = jnp.zeros((F, F), F32)
    for which in range(4):
        r, c = corner(s, which)
        part = jnp.where(touch_mask(which, r, c), value, 0.0)
        total += pltpu.roll(pltpu.roll(part, back_by(c), 1), back_by(r + s[CORE] * HALF), 0)
    keep[0] = total[:HALF]
    send[0] = total[HALF:]


def light_kernel(s, probe, out):
    power = probe[0] * probe[0] + probe[1] * probe[1]
    total = jnp.zeros((F, F), F32)
    for which in range(4):
        r, c = corner(s, which)
        part = pltpu.roll(pltpu.roll(power, r, 0), c, 1)
        total += jnp.where(touch_mask(which, r, c), part, 0.0)
    out[...] = total


def cut(obj, span, after=()):
    def kernel(obj, *refs):
        copy = pltpu.make_async_copy(obj.at[:, span[0] : span[1]], refs[-2], refs[-1])
        copy.start()
        copy.wait()

    return pl.pallas_call(
        kernel,
        out_shape=pltpu.VMEM((2, span[1] - span[0], F), F32),
        in_specs=[ANY] * (1 + len(after)),
        out_specs=VMEM,
        scratch_shapes=[pltpu.SemaphoreType.DMA],
        cost_estimate=pl.CostEstimate(flops=1, bytes_accessed=1, transcendentals=0),
    )(pltpu.with_memory_space_constraint(obj, pltpu.HBM), *after)


def column_mask(shape, col_at, odd, own):
    col = iota(shape, 1)
    return jnp.logical_xor(col >= col_at, odd if own else jnp.logical_not(odd))


def lend_kernel(span, s, tile, below, out):
    first, last = span
    row = iota((last - first, F), 0) + first
    for k in range(2):
        out[k] = jnp.where(row >= s[ROW_T], tile[k], below[k])


def half_kernel(span, s, tile, below, beside, turned, table, patch, half):
    first, last = span
    shape = (last - first, F)
    row = iota(shape, 0) + first
    here = column_mask(shape, s[COL], s[CORE] == 1, True)
    m = [
        jnp.where(here, jnp.where(row >= s[ROW], tile[k], below[k]), beside[k])
        for k in range(2)
    ]
    for k in range(2):
        patch[k] = m[k]
    p_re, p_im = turned[0, first:last], turned[1, first:last]
    psi_re = (p_re * m[0] - p_im * m[1]).astype(BF16)
    psi_im = (p_re * m[1] + p_im * m[0]).astype(BF16)
    psi = jnp.concatenate([psi_re, psi_im], axis=0)
    by_re = jnp.dot(psi, table[0], preferred_element_type=F32)
    by_im = jnp.dot(psi, table[1], preferred_element_type=F32)
    n = last - first
    half[0] = (by_re[:n] - by_im[n:]).astype(BF16)
    half[1] = (by_re[n:] + by_im[:n]).astype(BF16)


def pick_kernel(s, own, moved, out):
    out[...] = jnp.where(s[CORE] == 1, moved[...], own[...])


def dot_t(a, b):
    return lax.dot_general(a, b, (((1,), (1,)), ((), ())), preferred_element_type=F32)


def fourier_kernel(s, *refs):
    halves, patches = (refs[i * CHUNKS : (i + 1) * CHUNKS] for i in range(2))
    col_table, row_table, row_table_t, amps, turned = refs[2 * CHUNKS : 2 * CHUNKS + 5]
    grads, (keep, send, stack, change, back, numer) = refs[2 * CHUNKS + 5 :][:2], refs[2 * CHUNKS + 7 :]
    r, c = s[ROW], s[COL]
    for i, (first, last) in enumerate(SPANS):
        for k in range(2):
            stack[first:last, k * F : (k + 1) * F] = halves[i][k]
    wide = 256
    for j in range(0, F, wide):
        at = slice(j, j + wide)
        cols = jnp.concatenate([stack[:, at], stack[:, F + j : F + j + wide]], axis=1)
        by_re = jnp.dot(row_table_t[0], cols, preferred_element_type=F32)
        by_im = jnp.dot(row_table_t[1], cols, preferred_element_type=F32)
        re, im = by_re[:, :wide] - by_im[:, wide:], by_re[:, wide:] + by_im[:, :wide]
        factor = amps[0, :, at] / jnp.maximum(jnp.sqrt(re * re + im * im), 0.25) - 1.0
        change[:, :wide] = (factor * re).astype(BF16)
        change[:, wide:] = (factor * im).astype(BF16)
        by_re = jnp.dot(row_table[0], change[...], preferred_element_type=F32)
        by_im = jnp.dot(row_table[1], change[...], preferred_element_type=F32)
        back[0, :, at] = (by_re[:, :wide] + by_im[:, wide:]).astype(BF16)
        back[1, :, at] = (by_re[:, wide:] - by_im[:, :wide]).astype(BF16)
    tall = 128
    for j in range(0, F, tall):
        at = slice(j, j + tall)
        rows = jnp.concatenate([back[0, at], back[1, at]], axis=0)
        by_re, by_im = dot_t(rows, col_table[0]), dot_t(rows, col_table[1])
        re, im = by_re[:tall] + by_im[tall:], by_re[tall:] - by_im[:tall]
        p_re, p_im = turned[0, at], turned[1, at]
        grad, rows = next((g, slice(j - a, j - a + tall)) for g, (a, b) in zip(grads, OUT_SPANS) if j < b)
        grad[0, rows] = p_re * re + p_im * im
        grad[1, rows] = p_re * im - p_im * re
        for i, (first, last) in enumerate(SPANS):
            low, high = max(first, j), min(last, j + tall)
            if low < high:
                m_re, m_im = (patches[i][k, low - first : high - first] for k in range(2))
                e_re, e_im = re[low - j : high - j], im[low - j : high - j]
                numer[0, low:high] = pltpu.roll(m_re * e_re + m_im * e_im, back_by(c), 1)
                numer[1, low:high] = pltpu.roll(m_re * e_im - m_im * e_re, back_by(c), 1)
    for k in range(2):
        turned_back = pltpu.roll(numer[k], back_by(r + s[CORE] * HALF), 0)
        keep[k] = turned_back[:HALF]
        send[k] = turned_back[HALF:]


def fallen_masks(span, s, below):
    shape = (span[1] - span[0], F)
    row = iota(shape, 0) + span[0]
    odd = s[CORE] == 1
    rows = [row < s[at] if below else row >= s[at] for at in (ROW, ROW_T)]
    here = jnp.logical_and(column_mask(shape, s[COL], odd, True), rows[0])
    there = jnp.logical_and(column_mask(shape, s[COL_T], odd, False), rows[1])
    return here, there


def down_kernel(span, s, grad, moved, down):
    here, there = fallen_masks(span, s, True)
    for k in range(2):
        down[k] = jnp.where(here, grad[k], 0.0) + jnp.where(there, moved[k], 0.0)


def stay_kernel(s, obj, light, *refs):
    grads, moved, (base, scale) = refs[:2], refs[2:4], refs[4:]
    for i, span in enumerate(OUT_SPANS):
        at = slice(*span)
        here, there = fallen_masks(span, s, False)
        part = 1.0 / (light[at] + 1.0)
        scale[at] = part
        for k in range(2):
            stay = jnp.where(here, grads[i][k], 0.0) + jnp.where(there, moved[i][k], 0.0)
            base[k, at] = obj[k, at] + stay * part


def object_kernel(s, base, scale, *refs):
    fallen, (out, ready) = refs[:2], refs[2:]
    ready[...] = jnp.zeros(ready.shape, F32)
    for i, span in enumerate(OUT_SPANS):
        at = slice(*span)
        for k in range(2):
            out[k, at] = base[k, at] + fallen[i][k] * scale[at]


def turn(value, along, steps):
    if along == "z":
        return lax.ppermute(value, "obj", [(o, (o + 2 * steps) % (2 * Z)) for o in range(2 * Z)])
    pairs = []
    for y in range(Y):
        for x in range(X):
            to = (y, (x + steps) % X) if along == "x" else ((y + steps) % Y, x)
            pairs.append((y * X + x, to[0] * X + to[1]))
    return lax.ppermute(value, "pos", pairs)


def exchange(blocks, along):
    return [blocks[0]] + [turn(blocks[j], along, j) for j in range(1, 4)]


def block_rows(at, j, size):
    return pl.ds(pl.multiple_of(jnp.bitwise_and(at + j, 3) * size, size), size)


def share_kernel(s, keep, got, *outs):
    for j, out in enumerate(outs):
        rows = block_rows(s[AT_Z], j, QUARTER)
        out[...] = keep[:, rows, :] + got[:, rows, :]


def sum_kernel(s, *refs):
    numer, light, outs = refs[:4], refs[4:8], refs[8:]
    for j, out in enumerate(outs):
        rows = block_rows(s[AT_Y], j, BLOCK)
        for first, parts in ((0, numer), (2, light)):
            a, b, c, d = [ref[:, rows, :] for ref in parts]
            out[first : first + a.shape[0]] = a + b + c + d


def add_kernel(s, a, b, c, d, out):
    out[...] = a[...] + b[...] + c[...] + d[...]


def update_kernel(beta, s, a, b, c, d, probe, out):
    total = a[...] + b[...] + c[...] + d[...]
    out[...] = probe[...] + beta * total[:2] / (total[2:3] + 1.0)


def join_kernel(axis, s, *refs):
    for j in range(4):
        refs[4][jnp.bitwise_and(s[axis] - j, 3)] = refs[j][...]


def pair_kernel(s, mine, other, out):
    for ref, half in ((mine, s[CORE]), (other, 1 - s[CORE])):
        for z in range(Z):
            for y in range(Y):
                first = pl.multiple_of(half * HALF + (z * QUARTER + y * BLOCK), BLOCK)
                out[:, pl.ds(first, BLOCK), :] = ref[z, y]


def swap(value):
    return lax.ppermute(value, "obj", [(o, o ^ 1) for o in range(2 * Z)])


def shifted(value, steps):
    n = 2 * Z
    return lax.ppermute(value, "obj", [(o, o + steps) for o in range(n) if 0 <= o + steps < n])


def x_pairs(odd_only=False):
    n = Y * X
    pairs = [(o * n + p, o * n + (p + 1) % n) for o in range(1, 2 * Z, 2) for p in range(n)]
    if not odd_only:
        pairs += [(o * n + p, o * n + p - 1) for o in range(0, 2 * Z, 2) for p in range(1, n)]
    return pairs


def toward(value, odd_only=False):
    return lax.ppermute(value, ("obj", "pos"), x_pairs(odd_only))


def homeward(value):
    return lax.ppermute(value, ("obj", "pos"), [(b, a) for a, b in x_pairs()])


def body(object_field, probe, amplitudes, offsets):
    row_index = lax.axis_index("obj")
    col_index = lax.axis_index("pos")
    core, z, y = row_index % 2, row_index // 2, col_index // X
    place_here = jnp.stack([core, z, y])
    own = offsets[0] - jnp.stack([row_index * F, col_index * F])
    n = Y * X
    left = lax.ppermute(own, "pos", [(p, (p + 1) % n) for p in range(n)])
    above = shifted(jnp.concatenate([own, left]), 1)
    odd = core == 1
    mine, target = jnp.where(odd, left, own), jnp.where(odd, own, left)
    s = jnp.concatenate([mine, target, place_here]).astype(jnp.int32)
    touch = jnp.concatenate([s, own, left, above]).astype(jnp.int32)

    shapes = [((2, last - first, F), F32) for first, last in SPANS]

    tiles = [cut(object_field, SPANS[0]), cut(object_field, SPANS[1], (left,))]
    below = [shifted(tile, -1) for tile in tiles]
    amps_moved = toward(amplitudes, odd_only=True)
    lent, beside = [], []

    def lend(i, after):
        lent.extend(
            call(
                functools.partial(lend_kernel, SPANS[i]),
                [shapes[i]],
                (touch, tiles[i], below[i]),
                after=after,
                keep=jax.ShapeDtypeStruct,
            )
        )
        beside.append(toward(lent[i]))

    lend(0, ())
    seen, seen_send = call(
        probe_light_kernel,
        [((1, HALF, F), F32)] * 2,
        (touch, object_field),
        after=(lent[0], amps_moved),
        limit=16,
    )
    lend(1, (seen,))
    wr, wi = dft_tables()
    square = ((2, F, F), BF16)
    col_table, row_table, row_table_t, turned, probe_block = call(
        prep_kernel,
        [square] * 3 + [((2, F, F), F32), ((2, BLOCK, F), F32)],
        (s, wr, wi, probe),
        after=(lent[1],),
        limit=16,
        keep=jax.ShapeDtypeStruct,
    )
    seen = call(
        share_kernel, [((1, QUARTER, F), F32)] * 4, (s, seen, swap(seen_send)), after=(turned,)
    )
    seen = exchange(seen, "z")

    patches, halves = [], []
    for i, span in enumerate(SPANS):
        patch, half = call(
            functools.partial(half_kernel, span),
            [shapes[i], (shapes[i][0], BF16)],
            (s, tiles[i], below[i], beside[i], turned, col_table),
            after=(seen[0],) if i == 0 else (patches[-1], *seen, amps),
            limit=16,
            keep=jax.ShapeDtypeStruct,
        )
        patches.append(patch)
        halves.append(half)
        if i == 0:
            (amps,) = call(
                pick_kernel,
                [((1, F, F), F32)],
                (s, amplitudes, amps_moved),
                after=(patch,),
            )

    half_tile = ((2, HALF, F), F32)
    *grads, keep, send = call(
        fourier_kernel,
        [half_tile] * 2 + [((2, HALF, F), F32)] * 2,
        (s, *halves, *patches, col_table, row_table, row_table_t, amps, turned),
        limit=24,
        scratch=[
            pltpu.VMEM((F, 2 * F), BF16),
            pltpu.VMEM((F, F), BF16),
            pltpu.VMEM((2, F, F), BF16),
            pltpu.VMEM((2, F, F), F32),
        ],
    )

    quarter, block = ((2, QUARTER, F), F32), ((3, BLOCK, F), F32)
    parts = call(share_kernel, [quarter] * 4, (s, keep, swap(send)))
    moved = [homeward(grad) for grad in grads]
    (light,) = call(light_kernel, [((F, F), F32)], (touch, probe), after=(parts[0],), limit=16)
    (down,) = call(
        functools.partial(down_kernel, OUT_SPANS[0]), [half_tile], (s, grads[0], moved[0]), after=(light,)
    )
    fallen = [shifted(down, 1)]
    parts = call(sum_kernel, [block] * 4, (s, *exchange(parts, "z"), *seen), after=(down,))
    parts = exchange(parts, "y")
    (down,) = call(
        functools.partial(down_kernel, OUT_SPANS[1]), [half_tile], (s, grads[1], moved[1]), after=parts
    )
    fallen.append(shifted(down, 1))
    (share,) = call(add_kernel, [block], (s, *parts))
    beta = 0.5 * math.sqrt(2 * X * Y * Z)
    (fresh,) = call(
        functools.partial(update_kernel, beta),
        [((2, BLOCK, F), F32)],
        (s, *exchange([share] * 4, "x"), probe_block),
        after=(down,),
    )
    base, scale = call(
        stay_kernel,
        [((2, F, F), F32), ((F, F), F32)],
        (s, object_field, light, *grads, *moved),
        after=(share,),
    )
    (fresh,) = call(
        functools.partial(join_kernel, AT_Y),
        [((4,) + fresh.shape, F32)],
        (s, *exchange([fresh] * 4, "y")),
        after=(base,),
    )
    new_object, ready = call(
        object_kernel, [((2, F, F), F32), ((8, 128), F32)], (s, base, scale, *fallen), keep=pltpu.HBM
    )
    (fresh,) = call(
        functools.partial(join_kernel, AT_Z),
        [((4,) + fresh.shape, F32)],
        (s, *exchange([fresh] * 4, "z")),
        after=(ready,),
    )
    (new_probe,) = call(pair_kernel, [((2, F, F), F32)], (s, fresh, swap(fresh)), keep=pltpu.HBM)
    return (new_object, new_probe)


def solution(mesh):
    in_specs = (P(None, "obj", "pos"), P(), P(("obj", "pos"), None, None), P(("obj", "pos"), None))
    out_specs = (P(None, "obj", "pos"), P())
    return jax.shard_map(body, mesh=mesh, in_specs=in_specs, out_specs=out_specs, check_vma=False)
```
